32 devices in a mesh: seq: 8 (over z, x), tp: 4 (over y, core).
Axes of the slice: x: 2, y: 2, z: 4, core: 2. Of those that a mesh axis runs over, the one named last changes fastest.
Arguments:
- tokens: bfloat16 [16384, 1024], P('seq'), may hold values from -6 to 6
- cotangent: bfloat16 [16384, 1024], P('seq'), may hold values from -6 to 6
- start_flags: int32 [8], P('seq'), may hold values from 0 to 1, as said below
- gain_mixer: float32 [1024], replicated, may hold values from 0.5 to 1.5
- w_bgate: bfloat16 [1024, 1024], P(None, 'tp'), may hold values from -0.1875 to 0.1875
- w_cgate: bfloat16 [1024, 1024], P(None, 'tp'), may hold values from -0.1875 to 0.1875
- w_input: bfloat16 [1024, 1024], P(None, 'tp'), may hold values from -0.1875 to 0.1875
- conv_kernel: bfloat16 [3, 1024], P(None, 'tp'), may hold values from -3.5 to 3.5
- w_output: bfloat16 [1024, 1024], P('tp'), may hold values from -0.1875 to 0.1875
- gain_ffn: float32 [1024], replicated, may hold values from 0.5 to 1.5
- w_gate: bfloat16 [1024, 4608], P(None, 'tp'), may hold values from -0.1875 to 0.1875
- w_up: bfloat16 [1024, 4608], P(None, 'tp'), may hold values from -0.1875 to 0.1875
- w_down: bfloat16 [4608, 1024], P('tp'), may hold values from -0.09375 to 0.09375
- mean_gain_mixer: float32 [1024], replicated, may hold values from -16 to 16
- square_gain_mixer: float32 [1024], replicated, may hold values from 1 to 100
- mean_w_bgate: float32 [1024, 1024], P('seq', 'tp'), may hold values from -16 to 16
- square_w_bgate: float32 [1024, 1024], P('seq', 'tp'), may hold values from 1 to 100
- mean_w_cgate: float32 [1024, 1024], P('seq', 'tp'), may hold values from -16 to 16
- square_w_cgate: float32 [1024, 1024], P('seq', 'tp'), may hold values from 1 to 100
- mean_w_input: float32 [1024, 1024], P('seq', 'tp'), may hold values from -16 to 16
- square_w_input: float32 [1024, 1024], P('seq', 'tp'), may hold values from 1 to 100
- mean_conv_kernel: float32 [3, 1024], P(None, 'tp'), may hold values from -16 to 16
- square_conv_kernel: float32 [3, 1024], P(None, 'tp'), may hold values from 1 to 100
- mean_w_output: float32 [1024, 1024], P('tp', 'seq'), may hold values from -16 to 16
- square_w_output: float32 [1024, 1024], P('tp', 'seq'), may hold values from 1 to 100
- mean_gain_ffn: float32 [1024], replicated, may hold values from -16 to 16
- square_gain_ffn: float32 [1024], replicated, may hold values from 1 to 100
- mean_w_gate: float32 [1024, 4608], P('seq', 'tp'), may hold values from -16 to 16
- square_w_gate: float32 [1024, 4608], P('seq', 'tp'), may hold values from 1 to 100
- mean_w_up: float32 [1024, 4608], P('seq', 'tp'), may hold values from -16 to 16
- square_w_up: float32 [1024, 4608], P('seq', 'tp'), may hold values from 1 to 100
- mean_w_down: float32 [4608, 1024], P('tp', 'seq'), may hold values from -16 to 16
- square_w_down: float32 [4608, 1024], P('tp', 'seq'), may hold values from 1 to 100
Outputs:
- block_out: bfloat16 [16384, 1024], P('seq')
- grad_tokens: float32 [16384, 1024], P('seq')
- grad_gain_mixer: float32 [1024], replicated
- next_gain_mixer: float32 [1024], replicated
- mean_next_gain_mixer: float32 [1024], replicated
- square_next_gain_mixer: float32 [1024], replicated
- grad_w_bgate: float32 [1024, 1024], P('seq', 'tp')
- next_w_bgate: float32 [1024, 1024], P('seq', 'tp')
- mean_next_w_bgate: float32 [1024, 1024], P('seq', 'tp')
- square_next_w_bgate: float32 [1024, 1024], P('seq', 'tp')
- grad_w_cgate: float32 [1024, 1024], P('seq', 'tp')
- next_w_cgate: float32 [1024, 1024], P('seq', 'tp')
- mean_next_w_cgate: float32 [1024, 1024], P('seq', 'tp')
- square_next_w_cgate: float32 [1024, 1024], P('seq', 'tp')
- grad_w_input: float32 [1024, 1024], P('seq', 'tp')
- next_w_input: float32 [1024, 1024], P('seq', 'tp')
- mean_next_w_input: float32 [1024, 1024], P('seq', 'tp')
- square_next_w_input: float32 [1024, 1024], P('seq', 'tp')
- grad_conv_kernel: float32 [3, 1024], P(None, 'tp')
- next_conv_kernel: float32 [3, 1024], P(None, 'tp')
- mean_next_conv_kernel: float32 [3, 1024], P(None, 'tp')
- square_next_conv_kernel: float32 [3, 1024], P(None, 'tp')
- grad_w_output: float32 [1024, 1024], P('tp', 'seq')
- next_w_output: float32 [1024, 1024], P('tp', 'seq')
- mean_next_w_output: float32 [1024, 1024], P('tp', 'seq')
- square_next_w_output: float32 [1024, 1024], P('tp', 'seq')
- grad_gain_ffn: float32 [1024], replicated
- next_gain_ffn: float32 [1024], replicated
- mean_next_gain_ffn: float32 [1024], replicated
- square_next_gain_ffn: float32 [1024], replicated
- grad_w_gate: float32 [1024, 4608], P('seq', 'tp')
- next_w_gate: float32 [1024, 4608], P('seq', 'tp')
- mean_next_w_gate: float32 [1024, 4608], P('seq', 'tp')
- square_next_w_gate: float32 [1024, 4608], P('seq', 'tp')
- grad_w_up: float32 [1024, 4608], P('seq', 'tp')
- next_w_up: float32 [1024, 4608], P('seq', 'tp')
- mean_next_w_up: float32 [1024, 4608], P('seq', 'tp')
- square_next_w_up: float32 [1024, 4608], P('seq', 'tp')
- grad_w_down: float32 [4608, 1024], P('tp', 'seq')
- next_w_down: float32 [4608, 1024], P('tp', 'seq')
- mean_next_w_down: float32 [4608, 1024], P('tp', 'seq')
- square_next_w_down: float32 [4608, 1024], P('tp', 'seq')
The draws below stay inside these ranges and needn't reach their ends.
Inputs may be any that keep to these rules, and one draw needn't show every extreme that they name: `start_flags`: the first shard's flag is 1; shards 1 and 5 have flag 0, so they continue the sequence of the shard before them.
All inputs are finite; a program needn't handle non-finite values.
Results may differ from the reference program's by a relative error of at most 0.0075.
The reference program's roundings to bfloat16 on the way count: a program that leaves them out, or rounds other values in their place, can miss the bound.
Values sent between devices are 32-bit elements; how exact they have to be, the bound alone decides.
No kernel may reach another device: no remote copies, remote signals or barrier semaphores. Data moves between devices by JAX's collectives and lax.ppermute only.
A program may use at most 192 MiB of HBM per device.

```python
import math
import jax
import jax.numpy as jnp
from jax import lax

D = 1024
FF = 4608
KERNEL = 3
TOK_DEV = 2048
SHARDS = 8
TOKENS = 16384


def draw_start_flags(key, part):
    index = jnp.arange(SHARDS, dtype=jnp.int32)
    coins = jax.random.randint(jax.random.fold_in(key, 17), (SHARDS,), 0, 2, dtype=jnp.int32)
    middle = (index == 1) | (index == SHARDS // 2 + 1)
    return jnp.where(index == 0, 1, jnp.where(middle, 0, coins)).astype(jnp.int32)


def block_scale(stream_key, extent, cuts, low, top_value):
    loudness, own = 1.0, jax.random.fold_in(stream_key, 6)
    for dim, shards_of in cuts:
        steps = jnp.exp(jax.random.uniform(jax.random.fold_in(own, dim), (shards_of,), jnp.float32, low / len(cuts), top_value / len(cuts)))
        loudness = loudness * jnp.repeat(steps, extent[dim] // shards_of).reshape([-1 if axis == dim else 1 for axis in range(len(extent))])
    return loudness


def noise(key, dims, deviation, limit, cuts=(), held_as=jnp.bfloat16):
    drawn = jax.random.normal(key, dims, jnp.float32) * deviation
    if len(cuts) > 0:
        drawn = block_scale(key, dims, cuts, -0.22, 0.18) * drawn
    return jnp.clip(drawn, min=-limit, max=limit).astype(held_as)


def setup_inputs(seed: int = 0) -> dict:
    seeds = jax.random.split(jax.random.key(seed), 34)
    return {
        "tokens": noise(seeds[0], (TOKENS, D), 1.0, 6.0, ((0, 8),)),
        "cotangent": noise(seeds[1], (TOKENS, D), 1.0, 6.0, ((0, 8),)),
        "start_flags": draw_start_flags(jax.random.fold_in(seeds[33], 71), 0),
        "gain_mixer": jnp.clip(1.0 + 0.1 * jax.random.normal(seeds[3], (D,), jnp.float32), 0.5, 1.5),
        "w_bgate": noise(seeds[4], (D, D), D ** -0.5, 0.1875, ((1, 4),)),
        "w_cgate": noise(seeds[5], (D, D), D ** -0.5, 0.1875, ((1, 4),)),
        "w_input": noise(seeds[6], (D, D), D ** -0.5, 0.1875, ((1, 4),)),
        "conv_kernel": noise(seeds[7], (KERNEL, D), 3 ** -0.5, 3.5, ((1, 4),)),
        "w_output": noise(seeds[8], (D, D), D ** -0.5, 0.1875, ((0, 4),)),
        "gain_ffn": jnp.clip(1.0 + 0.1 * jax.random.normal(seeds[9], (D,), jnp.float32), 0.5, 1.5),
        "w_gate": noise(seeds[10], (D, FF), D ** -0.5, 0.1875, ((1, 4),)),
        "w_up": noise(seeds[11], (D, FF), D ** -0.5, 0.1875, ((1, 4),)),
        "w_down": noise(seeds[12], (FF, D), FF ** -0.5, 0.09375, ((0, 4),)),
        "mean_gain_mixer": noise(seeds[13], (D,), 3.0, 16.0, (), jnp.float32),
        "square_gain_mixer": jnp.clip(jnp.exp(jax.random.uniform(seeds[14], (D,), jnp.float32, math.log(1.0), math.log(100.0))), 1.0, 100.0),
        "mean_w_bgate": noise(seeds[15], (D, D), 3.0, 16.0, ((0, 8), (1, 4)), jnp.float32),
        "square_w_bgate": jnp.clip(jnp.exp(math.log(100.0) - 4.6051702 * jax.random.uniform(seeds[16], (D, D), jnp.float32) ** block_scale(seeds[16], (D, D), ((0, 8), (1, 4)), -0.2, 0.2)), 1.0, 100.0),
        "mean_w_cgate": noise(seeds[17], (D, D), 3.0, 16.0, ((0, 8), (1, 4)), jnp.float32),
        "square_w_cgate": jnp.clip(jnp.exp(math.log(100.0) - 4.6051702 * jax.random.uniform(seeds[18], (D, D), jnp.float32) ** block_scale(seeds[18], (D, D), ((0, 8), (1, 4)), -0.2, 0.2)), 1.0, 100.0),
        "mean_w_input": noise(seeds[19], (D, D), 3.0, 16.0, ((0, 8), (1, 4)), jnp.float32),
        "square_w_input": jnp.clip(jnp.exp(math.log(100.0) - 4.6051702 * jax.random.uniform(seeds[20], (D, D), jnp.float32) ** block_scale(seeds[20], (D, D), ((0, 8), (1, 4)), -0.2, 0.2)), 1.0, 100.0),
        "mean_conv_kernel": noise(seeds[21], (KERNEL, D), 3.0, 16.0, ((1, 4),), jnp.float32),
        "square_conv_kernel": jnp.clip(jnp.exp(math.log(100.0) - 4.6051702 * jax.random.uniform(seeds[22], (KERNEL, D), jnp.float32) ** block_scale(seeds[22], (KERNEL, D), ((1, 4),), -0.2, 0.2)), 1.0, 100.0),
        "mean_w_output": noise(seeds[23], (D, D), 3.0, 16.0, ((0, 4), (1, 8)), jnp.float32),
        "square_w_output": jnp.clip(jnp.exp(math.log(100.0) - 4.6051702 * jax.random.uniform(seeds[24], (D, D), jnp.float32) ** block_scale(seeds[24], (D, D), ((0, 4), (1, 8)), -0.2, 0.2)), 1.0, 100.0),
        "mean_gain_ffn": noise(seeds[25], (D,), 3.0, 16.0, (), jnp.float32),
        "square_gain_ffn": jnp.clip(jnp.exp(jax.random.uniform(seeds[26], (D,), jnp.float32, math.log(1.0), math.log(100.0))), 1.0, 100.0),
        "mean_w_gate": noise(seeds[27], (D, FF), 3.0, 16.0, ((0, 8), (1, 4)), jnp.float32),
        "square_w_gate": jnp.clip(jnp.exp(math.log(100.0) - 4.6051702 * jax.random.uniform(seeds[28], (D, FF), jnp.float32) ** block_scale(seeds[28], (D, FF), ((0, 8), (1, 4)), -0.2, 0.2)), 1.0, 100.0),
        "mean_w_up": noise(seeds[29], (D, FF), 3.0, 16.0, ((0, 8), (1, 4)), jnp.float32),
        "square_w_up": jnp.clip(jnp.exp(math.log(100.0) - 4.6051702 * jax.random.uniform(seeds[30], (D, FF), jnp.float32) ** block_scale(seeds[30], (D, FF), ((0, 8), (1, 4)), -0.2, 0.2)), 1.0, 100.0),
        "mean_w_down": noise(seeds[31], (FF, D), 3.0, 16.0, ((0, 4), (1, 8)), jnp.float32),
        "square_w_down": jnp.clip(jnp.exp(math.log(100.0) - 4.6051702 * jax.random.uniform(seeds[32], (FF, D), jnp.float32) ** block_scale(seeds[32], (FF, D), ((0, 4), (1, 8)), -0.2, 0.2)), 1.0, 100.0),
    }


@jax.custom_vjp
def low(v):
    return lax.optimization_barrier(v.astype(jnp.bfloat16)).astype(jnp.float32)

@jax.custom_vjp
def low_back(v):
    return v

def low_keep(v):
    return (low(v), None)

def low_pass(kept, grad):
    return (grad,)

def back_keep(v):
    return (v, None)

def back_low(kept, grad):
    return (low(grad),)
low.defvjp(low_keep, low_pass)
low_back.defvjp(back_keep, back_low)
EPS = 1e-05

def product(left, right):
    return jnp.dot(left, right, precision=lax.Precision.HIGHEST, preferred_element_type=jnp.float32)

def rms_scaled(values, gain):
    inverse = lax.rsqrt(lax.optimization_barrier(jnp.mean(values * values, axis=-1, keepdims=True)) + EPS)
    return values * inverse * gain

def adamw(weight, grad, mean, square, decay, rate):
    mean_new = 0.9 * mean + 0.1 * grad
    square_new = 0.95 * square + 0.05 * grad * grad
    mean_hat = mean_new / (1.0 - 0.9 ** 3)
    square_hat = square_new / (1.0 - 0.95 ** 3)
    weight_new = weight - rate * (mean_hat / (jnp.sqrt(square_hat) + 1e-08) + decay * weight)
    return (weight_new, mean_new, square_new)

def reference(tokens, cotangent, start_flags, gain_mixer, w_bgate, w_cgate, w_input, conv_kernel, w_output, gain_ffn, w_gate, w_up, w_down, mean_gain_mixer, square_gain_mixer, mean_w_bgate, square_w_bgate, mean_w_cgate, square_w_cgate, mean_w_input, square_w_input, mean_conv_kernel, square_conv_kernel, mean_w_output, square_w_output, mean_gain_ffn, square_gain_ffn, mean_w_gate, square_w_gate, mean_w_up, square_w_up, mean_w_down, square_w_down):
    rows = jnp.arange(TOKENS, dtype=jnp.int32)
    flagged = start_flags[rows // TOK_DEV] == 1
    place = rows % TOK_DEV
    keep_one = jnp.where(flagged & (place == 0), 0.0, 1.0).astype(jnp.float32)
    keep_two = jnp.where(flagged & (place < 2), 0.0, 1.0).astype(jnp.float32)
    block = math.gcd(TOKENS, 4096)
    count = TOKENS // block

    def forward(xin, gone, wbg, wcg, win, kern, wout, gtwo, wgt, wupp, wdwn):

        def layer(carry, pieces):
            rows_in, first, second = pieces
            hone = low(rms_scaled(rows_in, gone))
            bgate = low_back(product(hone, wbg))
            cgate = low_back(product(hone, wcg))
            xval = low_back(product(hone, win))
            mixed_in = bgate * xval
            extended = jnp.concatenate([carry, mixed_in], axis=0)
            conv = kern[2] * mixed_in + first[:, None] * kern[1] * extended[1:-1] + second[:, None] * kern[0] * extended[:-2]
            gated = low(cgate * conv)
            mix = low_back(product(gated, wout))
            resid = rows_in + mix
            htwo = low(rms_scaled(resid, gtwo))
            gate = low_back(product(htwo, wgt))
            upval = low_back(product(htwo, wupp))
            act = low(jax.nn.silu(gate) * upval)
            ffn = low_back(product(act, wdwn))
            return (mixed_in[-2:], resid + ffn)
        start = jnp.zeros((2, D), jnp.float32)
        _, outs = lax.scan(jax.checkpoint(layer), start, (xin.reshape(count, block, D), keep_one.reshape(count, block), keep_two.reshape(count, block)))
        return outs.reshape(TOKENS, D)
    params = [gain_mixer, w_bgate.astype(jnp.float32), w_cgate.astype(jnp.float32), w_input.astype(jnp.float32), conv_kernel.astype(jnp.float32), w_output.astype(jnp.float32), gain_ffn, w_gate.astype(jnp.float32), w_up.astype(jnp.float32), w_down.astype(jnp.float32)]
    result, pull = jax.vjp(forward, tokens.astype(jnp.float32), *params)
    grads = pull(cotangent.astype(jnp.float32))
    moments = [(mean_gain_mixer, square_gain_mixer), (mean_w_bgate, square_w_bgate), (mean_w_cgate, square_w_cgate), (mean_w_input, square_w_input), (mean_conv_kernel, square_conv_kernel), (mean_w_output, square_w_output), (mean_gain_ffn, square_gain_ffn), (mean_w_gate, square_w_gate), (mean_w_up, square_w_up), (mean_w_down, square_w_down)]
    decays = [0.0, 0.1, 0.1, 0.1, 0.1, 0.1, 0.0, 0.1, 0.1, 0.1]
    rates = [0.2, 0.01, 0.01, 0.01, 0.2, 0.01, 0.2, 0.01, 0.01, 0.01]
    outs = [result.astype(jnp.bfloat16), grads[0]]
    for index in range(10):
        grad = grads[index + 1]
        weight_new, mean_new, square_new = adamw(params[index], grad, moments[index][0], moments[index][1], decays[index], rates[index])
        outs = outs + [grad, weight_new, mean_new, square_new]
    return tuple(outs)
```

```python
import jax
import jax.numpy as jnp
from jax import lax
from jax.sharding import PartitionSpec as P

EPS = 1e-05


def shifted(block, axis, distance):
    devices = range(lax.axis_size(axis))
    route = [(i - distance, i) for i in devices if i - distance in devices]
    return lax.ppermute(block, axis, route)


def swap(block, axis, bit):
    return lax.ppermute(block, axis, [(i, i ^ bit) for i in range(lax.axis_size(axis))])


def swap_core(block):
    return swap(block, "tp", 1)


def swap_y(block):
    return swap(block, "tp", 2)


def narrow(block):
    one = 1.0 + (lax.axis_index("tp") // lax.axis_size("tp")).astype(jnp.float32)
    return (block * one).astype(jnp.bfloat16)


def wide(block):
    return block.astype(jnp.float32)


def dot(left, right):
    return jnp.dot(left, right, preferred_element_type=jnp.float32)


def inner_rows(left, right):
    return lax.dot_general(
        left, right, (((0,), (0,)), ((), ())), preferred_element_type=jnp.float32
    )


def times_back(left, right):
    return lax.dot_general(
        left, right, (((1,), (1,)), ((), ())), preferred_element_type=jnp.float32
    )


def adamw(weight, grad, mean, square, decay, rate):
    mean_new = 0.9 * mean + 0.1 * grad
    square_new = 0.95 * square + 0.05 * grad * grad
    mean_hat = mean_new / (1.0 - 0.9**3)
    square_hat = square_new / (1.0 - 0.95**3)
    weight_new = weight - rate * (mean_hat / (jnp.sqrt(square_hat) + 1e-08) + decay * weight)
    return (weight_new, mean_new, square_new)


def norm_back(dnormed, normed, inverse):
    return inverse * (dnormed - normed * jnp.mean(dnormed * normed, axis=-1, keepdims=True))


def log_two(number):
    bits = number.bit_length() - 1
    assert number == 1 << bits
    return bits


def scatter_rows(grad, place, order):
    shards = lax.axis_size("seq")
    width = grad.shape[0] // shards
    total = grad.reshape((shards, width) + grad.shape[1:])
    left = list(range(log_two(shards)))
    for bit in order:
        low = 1 << left.index(bit)
        pairs = total.reshape((-1, 2, low) + total.shape[1:])
        mine = (place >> bit) & 1
        send = lax.dynamic_index_in_dim(pairs, 1 - mine, 1, keepdims=False)
        keep = lax.dynamic_index_in_dim(pairs, mine, 1, keepdims=False)
        total = (keep + swap(send, "seq", 1 << bit)).reshape((-1,) + total.shape[1:])
        left.remove(bit)
    return total[0]


def sum_all(block, axis):
    for bit in range(log_two(lax.axis_size(axis))):
        block = block + swap(block, axis, 1 << bit)
    return block


def body(
    tokens,
    cotangent,
    start_flags,
    gain_mixer,
    w_bgate,
    w_cgate,
    w_input,
    conv_kernel,
    w_output,
    gain_ffn,
    w_gate,
    w_up,
    w_down,
    mean_gain_mixer,
    square_gain_mixer,
    mean_w_bgate,
    square_w_bgate,
    mean_w_cgate,
    square_w_cgate,
    mean_w_input,
    square_w_input,
    mean_conv_kernel,
    square_conv_kernel,
    mean_w_output,
    square_w_output,
    mean_gain_ffn,
    square_gain_ffn,
    mean_w_gate,
    square_w_gate,
    mean_w_up,
    square_w_up,
    mean_w_down,
    square_w_down,
):
    count, features = tokens.shape
    part = count // 4
    half = count // 2
    place = lax.axis_index("seq")
    rank = lax.axis_index("tp")
    upper = rank // 2
    near_first = list(range(log_two(lax.axis_size("seq"))))
    far_first = [near_first[1], near_first[0]] + near_first[2:]

    def rows(block, index, size):
        return lax.dynamic_slice_in_dim(block, index * size, size, 0)

    w_output_far = narrow(swap_y(wide(w_output)))
    w_output_both = jnp.concatenate([w_output, w_output_far], axis=0)
    xin = tokens.astype(jnp.float32)
    inverse_one = lax.rsqrt(jnp.mean(xin * xin, axis=-1, keepdims=True) + EPS)
    norm_one = xin * inverse_one
    hone = (norm_one * gain_mixer).astype(jnp.bfloat16)
    last = hone[-8:]
    mixed_last = dot(last, w_bgate) * dot(last, w_input)
    keeper = (1 - start_flags[0]).astype(jnp.float32)
    kernel = conv_kernel.astype(jnp.float32)
    previous = shifted(mixed_last[-2:], "seq", 1) * keeper
    bgate = dot(hone, w_bgate)
    cgate = dot(hone, w_cgate)
    xval = dot(hone, w_input)
    mixed_in = bgate * xval
    extended = jnp.concatenate([previous, mixed_in], axis=0)
    conv = kernel[2] * mixed_in + kernel[1] * extended[1:-1] + kernel[0] * extended[:-2]
    gated = (cgate * conv).astype(jnp.bfloat16)

    gated_far = narrow(swap_y(wide(rows(gated, 1 - upper, half))))
    gated_both = jnp.concatenate([rows(gated, upper, half), gated_far], axis=1)
    core = rank % 2
    mix_send = dot(rows(gated_both, 1 - core, part), w_output_both)
    mix_keep = dot(rows(gated_both, core, part), w_output_both)
    x_own = rows(tokens, rank, part).astype(jnp.float32)
    resid = x_own + (mix_keep + swap_core(mix_send))
    inverse_two = lax.rsqrt(jnp.mean(resid * resid, axis=-1, keepdims=True) + EPS)
    norm_two = resid * inverse_two
    htwo_own = (norm_two * gain_ffn).astype(jnp.bfloat16)

    sub = part // 2
    htwo_wide = wide(htwo_own)
    htwo_core = swap_core(htwo_wide)
    far = [swap_y(htwo_wide[:sub]), swap_y(htwo_wide[sub:])]
    cot = [rows(cotangent, rank ^ k, part) for k in range(4)]
    blocks = [
        (
            jnp.concatenate([htwo_own, narrow(htwo_core)], axis=0),
            jnp.concatenate([cot[0], cot[1]], axis=0),
        )
    ]
    for j in range(2):
        blocks.append(
            (
                jnp.concatenate([narrow(far[j]), narrow(swap_core(far[j]))], axis=0),
                jnp.concatenate(
                    [cot[2][j * sub : (j + 1) * sub], cot[3][j * sub : (j + 1) * sub]], axis=0
                ),
            )
        )
    acts, dgates, dups, ffns, dhtwos = [], [], [], [], []
    for htwo, cots in blocks:
        gate = dot(htwo, w_gate)
        upval = dot(htwo, w_up)
        sigma = jax.nn.sigmoid(gate)
        silu_gate = gate * sigma
        act = (silu_gate * upval).astype(jnp.bfloat16)
        dact = times_back(cots, w_down)
        dgate = (dact * upval * (sigma * (1.0 + gate * (1.0 - sigma)))).astype(jnp.bfloat16)
        dup = (dact * silu_gate).astype(jnp.bfloat16)
        acts.append(act)
        dgates.append(dgate)
        dups.append(dup)
        size = htwo.shape[0] // 2
        dsend = times_back(dgate[size:], w_gate) + times_back(dup[size:], w_up)
        dkeep = times_back(dgate[:size], w_gate) + times_back(dup[:size], w_up)
        dhtwos.append(dkeep + swap_core(dsend))
        fsend = dot(act[size:], w_down)
        fkeep = dot(act[:size], w_down)
        ffns.append(fkeep + swap_core(fsend))
    dhtwo = dhtwos[0] + jnp.concatenate([swap_y(dhtwos[1]), swap_y(dhtwos[2])], axis=0)
    ffn = ffns[0] + jnp.concatenate([swap_y(ffns[1]), swap_y(ffns[2])], axis=0)
    block_own = wide((resid + ffn).astype(jnp.bfloat16))

    def gather(own):
        beside = swap_core(own)
        across = swap_y(own)
        corner = swap_core(across)
        pieces = [own, beside, across, corner]
        whole = jnp.zeros((count, own.shape[1]), own.dtype)
        for k in range(4):
            whole = lax.dynamic_update_slice_in_dim(whole, pieces[k], (rank ^ k) * part, 0)
        return whole

    block_out = narrow(gather(block_own))

    htwo_all = jnp.concatenate([b[0] for b in blocks], axis=0)
    cot_all = jnp.concatenate([b[1] for b in blocks], axis=0)
    act_all = jnp.concatenate(acts, axis=0)
    dgate_all = jnp.concatenate(dgates, axis=0)
    dup_all = jnp.concatenate(dups, axis=0)
    grad_down = scatter_rows(inner_rows(cot_all, act_all), place, far_first)
    grad_gate = scatter_rows(inner_rows(htwo_all, dgate_all), place, near_first)
    grad_upw = scatter_rows(inner_rows(htwo_all, dup_all), place, near_first)

    gout = rows(cotangent, rank, part).astype(jnp.float32)
    dgain_ffn = jnp.sum(dhtwo * norm_two, axis=0)
    dresid = gout + norm_back(dhtwo * gain_ffn, norm_two, inverse_two)
    dmix_own = dresid.astype(jnp.bfloat16)
    dmix_core = narrow(swap_core(wide(dmix_own)))
    dmix = jnp.where(
        core == 0,
        jnp.concatenate([dmix_own, dmix_core], axis=0),
        jnp.concatenate([dmix_core, dmix_own], axis=0),
    )
    dgated_near = times_back(dmix, w_output)
    dgated_far = swap_y(times_back(dmix, w_output_far))
    dgated = jnp.where(
        upper == 0,
        jnp.concatenate([dgated_near, dgated_far], axis=0),
        jnp.concatenate([dgated_far, dgated_near], axis=0),
    )
    grad_outw_both = scatter_rows(inner_rows(dmix, gated_both), place, near_first)
    quarter = w_output.shape[0]
    grad_outw = (grad_outw_both[:, :quarter] + swap_y(grad_outw_both[:, quarter:])).T
    dcgate = (dgated * conv).astype(jnp.bfloat16)
    dconv = dgated * cgate
    dkernel = jnp.stack(
        [
            jnp.sum(dconv * extended[:-2], axis=0),
            jnp.sum(dconv * extended[1:-1], axis=0),
            jnp.sum(dconv * mixed_in, axis=0),
        ],
        axis=0,
    )
    dextended = (
        jnp.pad(kernel[2] * dconv, ((2, 0), (0, 0)))
        + jnp.pad(kernel[1] * dconv, ((1, 1), (0, 0)))
        + jnp.pad(kernel[0] * dconv, ((0, 2), (0, 0)))
    )
    returned = shifted(dextended[:2] * keeper, "seq", -1)
    dmixed = dextended[2:] + jnp.pad(returned, ((count - 2, 0), (0, 0)))
    dbgate = (dmixed * xval).astype(jnp.bfloat16)
    dxval = (dmixed * bgate).astype(jnp.bfloat16)
    dall = jnp.concatenate([dbgate, dcgate, dxval], axis=1)
    w_all = jnp.concatenate([w_bgate, w_cgate, w_input], axis=1)
    dparts = [times_back(rows(dall, rank ^ k, part), w_all) for k in (3, 2, 1, 0)]
    across = swap_y(dparts[1] + swap_core(dparts[0]))
    dhone = dparts[3] + swap_core(dparts[2]) + across
    grad_in = scatter_rows(inner_rows(hone, dall), place, near_first)
    inverse_own = lax.rsqrt(jnp.mean(x_own * x_own, axis=-1, keepdims=True) + EPS)
    norm_own = x_own * inverse_own
    dgain_mixer = jnp.sum(dhone * norm_own, axis=0)
    grad_own = dresid + norm_back(dhone * gain_mixer, norm_own, inverse_own)
    grad_tokens = gather(grad_own)

    gains = jnp.concatenate([dgain_mixer, dgain_ffn]).reshape(-1, 128)
    small = sum_all(jnp.concatenate([gains, dkernel.reshape(-1, 128)], axis=0), "seq")
    gains = sum_all(small[: gains.shape[0]], "tp").reshape(2, features)
    dkernel = small[gains.size // 128 :].reshape(dkernel.shape)

    width = features // lax.axis_size("seq")

    def rows_of(weight):
        return lax.dynamic_slice_in_dim(weight, place * width, width, 0).astype(jnp.float32)

    def columns_of(weight):
        return lax.dynamic_slice_in_dim(weight, place * width, width, 1).astype(jnp.float32)

    params = [
        gain_mixer,
        rows_of(w_bgate),
        rows_of(w_cgate),
        rows_of(w_input),
        kernel,
        columns_of(w_output),
        gain_ffn,
        rows_of(w_gate),
        rows_of(w_up),
        columns_of(w_down),
    ]
    grads = [
        gains[0],
        grad_in[:, :quarter],
        grad_in[:, quarter : 2 * quarter],
        grad_in[:, 2 * quarter :],
        dkernel,
        grad_outw,
        gains[1],
        grad_gate,
        grad_upw,
        grad_down.T,
    ]
    moments = [
        (mean_gain_mixer, square_gain_mixer),
        (mean_w_bgate, square_w_bgate),
        (mean_w_cgate, square_w_cgate),
        (mean_w_input, square_w_input),
        (mean_conv_kernel, square_conv_kernel),
        (mean_w_output, square_w_output),
        (mean_gain_ffn, square_gain_ffn),
        (mean_w_gate, square_w_gate),
        (mean_w_up, square_w_up),
        (mean_w_down, square_w_down),
    ]
    decays = [0.0, 0.1, 0.1, 0.1, 0.1, 0.1, 0.0, 0.1, 0.1, 0.1]
    rates = [0.2, 0.01, 0.01, 0.01, 0.2, 0.01, 0.2, 0.01, 0.01, 0.01]
    outs = [block_out, grad_tokens]
    for index in range(10):
        weight_new, mean_new, square_new = adamw(
            params[index],
            grads[index],
            moments[index][0],
            moments[index][1],
            decays[index],
            rates[index],
        )
        outs = outs + [grads[index], weight_new, mean_new, square_new]
    return tuple(outs)


def solution(mesh):
    in_specs = (
        P("seq", None),
        P("seq", None),
        P("seq"),
        P(),
        P(None, "tp"),
        P(None, "tp"),
        P(None, "tp"),
        P(None, "tp"),
        P("tp", None),
        P(),
        P(None, "tp"),
        P(None, "tp"),
        P("tp", None),
        P(),
        P(),
        P("seq", "tp"),
        P("seq", "tp"),
        P("seq", "tp"),
        P("seq", "tp"),
        P("seq", "tp"),
        P("seq", "tp"),
        P(None, "tp"),
        P(None, "tp"),
        P("tp", "seq"),
        P("tp", "seq"),
        P(),
        P(),
        P("seq", "tp"),
        P("seq", "tp"),
        P("seq", "tp"),
        P("seq", "tp"),
        P("tp", "seq"),
        P("tp", "seq"),
    )
    out_specs = (
        P("seq", None),
        P("seq", None),
        P(),
        P(),
        P(),
        P(),
        P("seq", "tp"),
        P("seq", "tp"),
        P("seq", "tp"),
        P("seq", "tp"),
        P("seq", "tp"),
        P("seq", "tp"),
        P("seq", "tp"),
        P("seq", "tp"),
        P("seq", "tp"),
        P("seq", "tp"),
        P("seq", "tp"),
        P("seq", "tp"),
        P(None, "tp"),
        P(None, "tp"),
        P(None, "tp"),
        P(None, "tp"),
        P("tp", "seq"),
        P("tp", "seq"),
        P("tp", "seq"),
        P("tp", "seq"),
        P(),
        P(),
        P(),
        P(),
        P("seq", "tp"),
        P("seq", "tp"),
        P("seq", "tp"),
        P("seq", "tp"),
        P("seq", "tp"),
        P("seq", "tp"),
        P("seq", "tp"),
        P("seq", "tp"),
        P("tp", "seq"),
        P("tp", "seq"),
        P("tp", "seq"),
        P("tp", "seq"),
    )
    return jax.shard_map(body, mesh=mesh, in_specs=in_specs, out_specs=out_specs, check_vma=False)
```

```python
import functools

import jax
import jax.numpy as jnp
from jax import lax
from jax.experimental import pallas as pl
from jax.experimental.pallas import tpu as pltpu
from jax.sharding import PartitionSpec as P

EPS = 1e-05


def shifted(block, axis, distance):
    devices = range(lax.axis_size(axis))
    route = [(i - distance, i) for i in devices if i - distance in devices]
    return lax.ppermute(block, axis, route)


def swap(block, axis, bit):
    return lax.ppermute(block, axis, [(i, i ^ bit) for i in range(lax.axis_size(axis))])


def swap_core(block):
    return swap(block, "tp", 1)


def swap_core_halves(block):
    size = block.shape[0] // 2
    return jnp.concatenate([swap_core(block[:size]), swap_core(block[size:])], axis=0)


class Clock:
    def __init__(self, value):
        self.value = value

    def passes(self, *values):
        values, self.value = lax.optimization_barrier((values, self.value))
        return values if len(values) > 1 else values[0]


def swap_y(block):
    return swap(block, "tp", 2)


def narrow(block):
    one = 1.0 + (lax.axis_index("tp") // lax.axis_size("tp")).astype(jnp.float32)
    return (block * one).astype(jnp.bfloat16)


def wide(block):
    return block.astype(jnp.float32)


def dot(left, right):
    return jnp.dot(left, right, preferred_element_type=jnp.float32)


def inner_rows(left, right):
    return lax.dot_general(
        left, right, (((0,), (0,)), ((), ())), preferred_element_type=jnp.float32
    )


def times_back(left, right):
    return lax.dot_general(
        left, right, (((1,), (1,)), ((), ())), preferred_element_type=jnp.float32
    )


def adamw(weight, grad, mean, square, decay, rate):
    mean_new = 0.9 * mean + 0.1 * grad
    square_new = 0.95 * square + 0.05 * grad * grad
    mean_hat = mean_new / (1.0 - 0.9**3)
    square_hat = square_new / (1.0 - 0.95**3)
    weight_new = weight - rate * (mean_hat / (jnp.sqrt(square_hat) + 1e-08) + decay * weight)
    return (weight_new, mean_new, square_new)


def norm_back(dnormed, normed, inverse):
    return inverse * (dnormed - normed * jnp.mean(dnormed * normed, axis=-1, keepdims=True))


def log_two(number):
    bits = number.bit_length() - 1
    assert number == 1 << bits
    return bits


def ffn_kernel(count, place, *refs):
    pieces, (cotangent, *weights) = refs[:count], refs[count : count + 4]
    outs, scratch = refs[-15:-7], refs[-7:]
    htwo_out, act_out, dgate_out, dup_out, fkeep, fsend, dkeep, dsend = outs
    w_gate, w_up, w_down, cots, htwo, weight_sems, cot_sems = scratch
    step = pl.program_id(0)
    size = htwo.shape[0]
    copies = [
        pltpu.make_async_copy(source, target, weight_sems.at[k])
        for k, (source, target) in enumerate(zip(weights, (w_gate, w_up, w_down)))
    ]

    def cot_copy(index):
        rows = pl.ds(pl.multiple_of(place[index] * size, size), size)
        slot = index % 2
        return pltpu.make_async_copy(cotangent.at[rows], cots.at[slot], cot_sems.at[slot])

    @pl.when(step == 0)
    def _():
        copies[0].start()
        copies[1].start()
        cot_copy(0).start()
        copies[2].start()

    @pl.when(step + 1 < count)
    def _():
        cot_copy(step + 1).start()

    for k, ref in enumerate(pieces):

        @pl.when(step == k)
        def _(ref=ref):
            htwo[...] = ref[...].astype(jnp.bfloat16)

    htwo_out[...] = htwo[...]

    @pl.when(step == 0)
    def _():
        copies[0].wait()

    gate = dot(htwo[...], w_gate[...])

    @pl.when(step == 0)
    def _():
        copies[1].wait()

    upval = dot(htwo[...], w_up[...])
    cot_copy(step).wait()

    @pl.when(step == 0)
    def _():
        copies[2].wait()

    dact = times_back(cots[step % 2], w_down[...])
    sigma = jax.nn.sigmoid(gate)
    silu_gate = gate * sigma
    act = (silu_gate * upval).astype(jnp.bfloat16)
    dgate = (dact * upval * (sigma * (1.0 + gate * (1.0 - sigma)))).astype(jnp.bfloat16)
    dup = (dact * silu_gate).astype(jnp.bfloat16)
    act_out[...] = act
    dgate_out[...] = dgate
    dup_out[...] = dup
    dhtwo = times_back(dgate, w_gate[...]) + times_back(dup, w_up[...])
    ffn = dot(act, w_down[...])

    @pl.when(step % 2 == 0)
    def _():
        fkeep[...] = ffn
        dkeep[...] = dhtwo

    @pl.when(step % 2 == 1)
    def _():
        fsend[...] = ffn
        dsend[...] = dhtwo


def feed_forward(place, pieces, cotangent, weights, kept):
    features = cotangent.shape[1]
    size = pieces[0].shape[0]
    units = weights[0].shape[1]
    whole = lambda ref: pl.BlockSpec(ref.shape, lambda i, p: (0, 0), pipeline_mode=pl.Buffered(1))
    spot = lambda width: pl.BlockSpec((size, width), lambda i, p: (p[i], 0))
    part = pl.BlockSpec((size, features), lambda i, p: (i // 2, 0))
    kept = [] if kept is None else list(kept)
    shapes = [
        pltpu.HBM((cotangent.shape[0], width), jnp.bfloat16)
        for width in (features, units, units, units)
    ]
    shapes += [pltpu.HBM((size * len(pieces) // 2, features), jnp.float32)] * 4
    return pl.pallas_call(
        functools.partial(ffn_kernel, len(pieces)),
        grid_spec=pltpu.PrefetchScalarGridSpec(
            num_scalar_prefetch=1,
            grid=(len(pieces),),
            in_specs=[whole(ref) for ref in pieces]
            + [pl.BlockSpec(memory_space=pltpu.HBM)] * 4
            + [pl.BlockSpec(memory_space=pl.ANY)] * len(kept),
            out_specs=[spot(features), spot(units), spot(units), spot(units)] + [part] * 4,
            scratch_shapes=[pltpu.VMEM(w.shape, w.dtype) for w in weights]
            + [
                pltpu.VMEM((2, size, features), cotangent.dtype),
                pltpu.VMEM((size, features), jnp.bfloat16),
                pltpu.SemaphoreType.DMA((3,)),
                pltpu.SemaphoreType.DMA((2,)),
            ],
        ),
        out_shape=shapes,
        input_output_aliases={5 + len(pieces) + i: i for i in range(len(kept))},
        compiler_params=pltpu.CompilerParams(vmem_limit_bytes=57 * 2**20),
        cost_estimate=pl.CostEstimate(flops=3 * 10**10, bytes_accessed=10**7, transcendentals=0),
    )(jnp.stack(place).astype(jnp.int32), *pieces, cotangent, *weights, *kept)


def place_kernel(pieces, spots, *refs):
    out = refs[-1]
    size = out.shape[0]
    for step, (index, part) in enumerate(pieces):

        @pl.when(pl.program_id(0) == step)
        def _(step=step, index=index, part=part):
            out[...] = refs[index][part * size : (part + 1) * size, :].astype(out.dtype)


def place_rows(blocks, spots, size, count, dtype, whole=None):
    width = blocks[0].shape[1]
    held = [] if whole is None else [whole]
    pieces = [(k, i) for k, block in enumerate(blocks) for i in range(block.shape[0] // size)]
    return pl.pallas_call(
        functools.partial(place_kernel, pieces),
        grid_spec=pltpu.PrefetchScalarGridSpec(
            num_scalar_prefetch=1,
            grid=(len(pieces),),
            in_specs=[
                pl.BlockSpec(block.shape, lambda i, p: (0, 0), pipeline_mode=pl.Buffered(1))
                for block in blocks
            ]
            + [pl.BlockSpec(memory_space=pl.ANY)] * len(held),
            out_specs=pl.BlockSpec((size, width), lambda i, p: (p[i], 0)),
        ),
        out_shape=jax.ShapeDtypeStruct((count, width), dtype),
        input_output_aliases={1 + len(blocks): 0} if held else {},
        compiler_params=pltpu.CompilerParams(vmem_limit_bytes=32 * 2**20),
        cost_estimate=pl.CostEstimate(
            flops=0, bytes_accessed=8 * len(pieces) * size * width, transcendentals=0
        ),
    )(jnp.stack(spots).astype(jnp.int32), *blocks, *held)


def sum_kernel(wide_rows, parts, picks, *refs):
    right, send, keep = refs[parts], refs[-2], refs[-1]
    left = jnp.concatenate([ref[...] for ref in refs[:parts]], axis=1)
    total = inner_rows(left, right[...])

    @pl.when(pl.program_id(0) == 0)
    def _():
        send[...] = total

    @pl.when(pl.program_id(0) == 1)
    def _():
        keep[...] = total


def sum_halves(left, right, place, bit):
    shards = lax.axis_size("seq")
    width = left.shape[1] // shards
    parts = shards // 2
    mine = (place >> bit) & 1
    low = jnp.arange(parts, dtype=jnp.int32)
    low, high = low & ((1 << bit) - 1), low >> bit
    base = (high << (bit + 1)) | low
    picks = jnp.concatenate([base | ((1 - mine) << bit), base | (mine << bit)]).astype(jnp.int32)
    if width % 128 != 0:
        total = inner_rows(left, right).reshape(-1, 2, 1 << bit, width * right.shape[1])
        return tuple(
            lax.dynamic_index_in_dim(total, which, 1, keepdims=False).reshape(-1, right.shape[1])
            for which in (1 - mine, mine)
        )
    count, units = right.shape
    half = jax.ShapeDtypeStruct((parts * width, units), jnp.float32)
    pick = lambda k: pl.BlockSpec((count, width), lambda i, p, k=k: (0, p[i * parts + k]))
    fixed = lambda shape: pl.BlockSpec(shape, lambda i, p: (0, 0), pipeline_mode=pl.Buffered(1))
    return pl.pallas_call(
        functools.partial(sum_kernel, width, parts),
        grid_spec=pltpu.PrefetchScalarGridSpec(
            num_scalar_prefetch=1,
            grid=(2,),
            in_specs=[pick(k) for k in range(parts)] + [fixed(right.shape)],
            out_specs=[fixed(half.shape)] * 2,
        ),
        out_shape=[pltpu.HBM(half.shape, half.dtype)] * 2,
        compiler_params=pltpu.CompilerParams(vmem_limit_bytes=57 * 2**20),
        cost_estimate=pl.CostEstimate(flops=10**12, bytes_accessed=10**7, transcendentals=0),
    )(picks, *[left] * parts, right)


def step_kernel(picks, *refs):
    keep_one, came_one, keep_two, came_two, send, keep = refs
    send[...] = keep_one[...] + came_one[...]
    keep[...] = keep_two[...] + came_two[...]


def halve_sum(kept, came, mine, low):
    blocks, width, units = kept.shape
    if width % 8 != 0 or units % 128 != 0:
        pairs = (kept + came).reshape(-1, 2, low, width, units)
        return tuple(
            lax.dynamic_index_in_dim(pairs, which, 1, keepdims=False).reshape(-1, width, units)
            for which in (1 - mine, mine)
        )
    index = jnp.arange(blocks // 2, dtype=jnp.int32)
    base = (index // low) * (2 * low) + index % low
    picks = jnp.concatenate([base + (1 - mine) * low, base + mine * low]).astype(jnp.int32)
    one = pl.BlockSpec((1, width, units), lambda i, p: (p[i], 0, 0))
    two = pl.BlockSpec((1, width, units), lambda i, p: (p[i + blocks // 2], 0, 0))
    half = pl.BlockSpec((1, width, units), lambda i, p: (i, 0, 0))
    return pl.pallas_call(
        step_kernel,
        grid_spec=pltpu.PrefetchScalarGridSpec(
            num_scalar_prefetch=1,
            grid=(blocks // 2,),
            in_specs=[one, one, two, two],
            out_specs=[half, half],
        ),
        out_shape=[jax.ShapeDtypeStruct((blocks // 2, width, units), kept.dtype)] * 2,
        cost_estimate=pl.CostEstimate(flops=10**12, bytes_accessed=10**7, transcendentals=0),
    )(picks, kept, came, kept, came)


class Halving:
    def __init__(self, clock, left, right, place, order):
        shards = lax.axis_size("seq")
        self.shape = (left.shape[1] // shards, right.shape[1])
        self.place = place
        self.order = list(order)
        self.left = list(range(log_two(shards)))
        left, right = clock.passes(left, right)
        send, keep = clock.passes(*sum_halves(left, right, place, order[0]))
        self.send, self.keep = send.reshape((-1,) + self.shape), keep.reshape((-1,) + self.shape)

    def start(self, clock=None):
        bit = self.order.pop(0)
        self.left.remove(bit)
        send = self.send if clock is None else clock.passes(self.send)
        self.came = swap(send, "seq", 1 << bit)

    def finish(self, clock):
        came = clock.passes(self.came)
        if not self.order:
            self.total = self.keep + came
            return
        bit = self.order[0]
        low = 1 << self.left.index(bit)
        self.send, self.keep = halve_sum(self.keep, came, (self.place >> bit) & 1, low)

    def final(self, clock):
        self.finish(clock)
        while self.order:
            self.start()
            self.finish(clock)
        return self.total[0]


def sum_all(block, axis):
    for bit in range(log_two(lax.axis_size(axis))):
        block = block + swap(block, axis, 1 << bit)
    return block


def body(
    tokens,
    cotangent,
    start_flags,
    gain_mixer,
    w_bgate,
    w_cgate,
    w_input,
    conv_kernel,
    w_output,
    gain_ffn,
    w_gate,
    w_up,
    w_down,
    mean_gain_mixer,
    square_gain_mixer,
    mean_w_bgate,
    square_w_bgate,
    mean_w_cgate,
    square_w_cgate,
    mean_w_input,
    square_w_input,
    mean_conv_kernel,
    square_conv_kernel,
    mean_w_output,
    square_w_output,
    mean_gain_ffn,
    square_gain_ffn,
    mean_w_gate,
    square_w_gate,
    mean_w_up,
    square_w_up,
    mean_w_down,
    square_w_down,
):
    count, features = tokens.shape
    half = count // 2
    part = count // 4
    sub = count // 8
    place = lax.axis_index("seq")
    rank = lax.axis_index("tp")
    upper = rank // 2
    core = rank % 2
    near_first = list(range(log_two(lax.axis_size("seq"))))
    far_first = [near_first[1], near_first[0]] + near_first[2:]
    quarter = w_output.shape[0]

    def rows(block, index, size):
        return lax.dynamic_slice_in_dim(block, index * size, size, 0)

    def piece(chip, j, which):
        return chip * 4 + j * 2 + which

    def joined(mine, other):
        return jnp.where(
            core == 0,
            jnp.concatenate([mine, other], axis=0),
            jnp.concatenate([other, mine], axis=0),
        )

    clock = Clock(gain_mixer)
    w_output_far = narrow(swap_y(wide(w_output)))
    w_output_both = jnp.concatenate([w_output, w_output_far], axis=0)
    xin = tokens.astype(jnp.float32)
    inverse_one = lax.rsqrt(jnp.mean(xin * xin, axis=-1, keepdims=True) + EPS)
    norm_one = xin * inverse_one
    hone = (norm_one * gain_mixer).astype(jnp.bfloat16)
    last = hone[-8:]
    mixed_last = dot(last, w_bgate) * dot(last, w_input)
    cgate_next = shifted(dot(hone[:8], w_cgate), "seq", -1)
    keeper = (1 - start_flags[0]).astype(jnp.float32)
    kernel = conv_kernel.astype(jnp.float32)
    previous = shifted(mixed_last, "seq", 1)[-2:] * keeper
    bgate = dot(hone, w_bgate)
    cgate = dot(hone, w_cgate)
    xval = dot(hone, w_input)
    mixed_in = bgate * xval
    extended = jnp.concatenate([previous, mixed_in], axis=0)
    conv = kernel[2] * mixed_in + kernel[1] * extended[1:-1] + kernel[0] * extended[:-2]
    gated = (cgate * conv).astype(jnp.bfloat16)

    gated_both, resid, norm_two, inverse_two, htwo_own, htwo_near = [], [], [], [], [], []
    htwo_across = []
    w_all = jnp.concatenate([w_bgate, w_cgate, w_input], axis=1)
    x_own = [
        rows(tokens, piece(upper, j, core), sub).astype(jnp.float32) for j in range(2)
    ]
    inverse_own = [
        lax.rsqrt(jnp.mean(x * x, axis=-1, keepdims=True) + EPS) for x in x_own
    ]
    far = swap_y(wide(rows(gated, 1 - upper, half)))
    w_all = jnp.concatenate([w_all, narrow(swap_core(wide(w_all)))], axis=1)
    w_all, inverse_own, w_output_far, w_output_both, cgate_next = clock.passes(
        w_all, inverse_own, w_output_far, w_output_both, cgate_next
    )
    far = clock.passes(far)
    fars = [far[:part], far[part:]]
    for j in range(2):
        both = jnp.concatenate([rows(gated, upper * 2 + j, part), narrow(fars[j])], axis=1)
        gated_both.append(both)
        mix_send = dot(rows(both, 1 - core, sub), w_output_both)
        mix_keep = dot(rows(both, core, sub), w_output_both)
        resid.append(x_own[j] + (mix_keep + swap_core(mix_send)))
        inverse_two.append(
            lax.rsqrt(jnp.mean(resid[j] * resid[j], axis=-1, keepdims=True) + EPS)
        )
        norm_two.append(resid[j] * inverse_two[j])
        htwo_own.append(wide((norm_two[j] * gain_ffn).astype(jnp.bfloat16)))
        htwo_across.append(swap_y(htwo_own[j]))
        htwo_near.append(swap_core(htwo_own[j]))

    weights = (w_gate, w_up, w_down)
    spots = [piece(upper, j, which) for j in range(2) for which in (core, 1 - core)]
    pieces = [v for j in range(2) for v in (htwo_own[j], htwo_near[j])]
    outs = clock.passes(*feed_forward(spots, pieces, cotangent, weights, None))
    kept, ffn_here, dhtwo_here = outs[:4], outs[4:6], outs[6:]
    ffn_there, dhtwo_across = [], []
    dhtwo_here = dhtwo_here[0] + swap_core(dhtwo_here[1])
    for j in range(2):
        if j == 1:
            dhtwo_here = clock.passes(dhtwo_here)
        across = clock.passes(htwo_across[j])
        spots = [piece(1 - upper, j, which) for which in (core, 1 - core)]
        pieces = [across, swap_core(across)]
        outs = clock.passes(*feed_forward(spots, pieces, cotangent, weights, kept))
        kept = outs[:4]
        ffn_there.append(outs[4:6])
        dhtwo_across.append(swap_y(clock.passes(outs[6] + swap_core_halves(outs[7]))))
    htwo_all, act_all, dgate_all, dup_all = kept
    def to_previous(block, chip):
        ranks = lax.axis_size("tp")
        route = [
            (s * ranks + c, (s - 1) * ranks + 2 * chip + c)
            for s in range(1, lax.axis_size("seq"))
            for c in range(2)
        ]
        return lax.ppermute(block, ("seq", "tp"), route)

    dresid, dgain_ffn, dmix, dgated_near, dgated_far = [], 0.0, [], [], []

    def before_swap(j):
        gout = rows(cotangent, piece(upper, j, core), sub).astype(jnp.float32)
        dhtwo = dhtwo_here[j * sub : (j + 1) * sub] + clock.passes(dhtwo_across[j])
        dresid.append(gout + norm_back(dhtwo * gain_ffn, norm_two[j], inverse_two[j]))
        dmix_own = clock.passes(wide(dresid[j].astype(jnp.bfloat16)))
        return dmix_own, swap_core(dmix_own), jnp.sum(dhtwo * norm_two[j], axis=0)

    def after_swap(dmix_own, came):
        dmix.append(narrow(joined(dmix_own, clock.passes(came))))
        near, far = clock.passes(
            times_back(dmix[-1], w_output), times_back(dmix[-1], w_output_far)
        )
        dgated_near.append(near)
        dgated_far.append(swap_y(far))
        return near, far

    def ffn_sum(j):
        keep, send = clock.passes(*ffn_there[j])
        return keep + swap_core(send)

    dmix_own, came, gain_part = before_swap(0)
    dgain_ffn = dgain_ffn + gain_part
    down = Halving(clock, cotangent, act_all, place, far_first)
    near, far = after_swap(dmix_own, came)
    dgated_next = to_previous(near[:8] * keeper, 0) + to_previous(far[:8] * keeper, 1)
    gate = Halving(clock, htwo_all, dgate_all, place, near_first)
    down.start(clock)
    gate.start(clock)
    dgated_next = clock.passes(dgated_next)
    dmix_own, came, gain_part = before_swap(1)
    dgain_ffn = dgain_ffn + gain_part
    dgated_far[0] = clock.passes(dgated_far[0])
    ffn_far = [ffn_sum(j) for j in range(2)]
    upw = Halving(clock, htwo_all, dup_all, place, near_first)
    after_swap(dmix_own, came)
    ffn_across = [swap_y(clock.passes(block)) for block in ffn_far]
    outw = Halving(
        clock,
        jnp.concatenate(dmix, axis=0),
        jnp.concatenate(gated_both, axis=0),
        place,
        near_first,
    )
    dgated_far[1] = clock.passes(dgated_far[1])
    dgated = jnp.where(
        upper == 0,
        jnp.concatenate(dgated_near + dgated_far, axis=0),
        jnp.concatenate(dgated_far + dgated_near, axis=0),
    )

    dcgate = (dgated * conv).astype(jnp.bfloat16)
    dconv = dgated * cgate
    dkernel = jnp.stack(
        [
            jnp.sum(dconv * extended[:-2], axis=0),
            jnp.sum(dconv * extended[1:-1], axis=0),
            jnp.sum(dconv * mixed_in, axis=0),
        ],
        axis=0,
    )
    dextended = (
        jnp.pad(kernel[2] * dconv, ((2, 0), (0, 0)))
        + jnp.pad(kernel[1] * dconv, ((1, 1), (0, 0)))
        + jnp.pad(kernel[0] * dconv, ((0, 2), (0, 0)))
    )
    dconv_next = dgated_next[:2] * cgate_next[:2]
    returned = jnp.concatenate(
        [kernel[0] * dconv_next[:1], kernel[1] * dconv_next[:1] + kernel[0] * dconv_next[1:]],
        axis=0,
    )
    dmixed = dextended[2:] + jnp.pad(returned, ((count - 2, 0), (0, 0)))
    dbgate = (dmixed * xval).astype(jnp.bfloat16)
    dxval = (dmixed * bgate).astype(jnp.bfloat16)
    dall = jnp.concatenate([dbgate, dcgate, dxval], axis=1)
    by_core = dall.reshape(4, 2, sub, dall.shape[1])
    send = lax.dynamic_index_in_dim(by_core, 1 - core, 1, keepdims=False)
    came = swap_core(clock.passes(wide(send)))
    down.finish(clock)
    gate.finish(clock)
    upw.start(clock)
    gate.start(clock)
    inw = Halving(clock, hone, dall, place, near_first)
    came = clock.passes(came)
    ffn_here = clock.passes(*ffn_here)
    ffn_near = swap_core(ffn_here[1])
    dall_own = lax.dynamic_index_in_dim(by_core, core, 1, keepdims=False)
    dall_own = jnp.concatenate([dall_own, narrow(came)], axis=2)

    def back_rows(chip, j):
        block = lax.dynamic_index_in_dim(dall_own, chip * 2 + j, 0, keepdims=False)
        return times_back(block, w_all)

    dhone_across = [swap_y(clock.passes(back_rows(1 - upper, j))) for j in range(2)]
    dhone_near = [back_rows(upper, j) for j in range(2)]

    ffn_across[0] = clock.passes(ffn_across[0])
    gate.finish(clock)
    gate.start(clock)
    ffn_near = ffn_here[0] + clock.passes(ffn_near)
    dgain_mixer, grads_own, grads_across = 0.0, [], []

    def arrives(j):
        norm_own = x_own[j] * inverse_own[j]
        dhone = dhone_near[j] + clock.passes(dhone_across[j])
        grad_own = dresid[j] + norm_back(dhone * gain_mixer, norm_own, inverse_own[j])
        grads_own.append(grad_own)
        return jnp.sum(dhone * norm_own, axis=0)

    ffn_across[1] = clock.passes(ffn_across[1])
    ffn = ffn_near + jnp.concatenate(ffn_across, axis=0)
    block_own = wide((jnp.concatenate(resid, axis=0) + ffn).astype(jnp.bfloat16))
    dgain_mixer = dgain_mixer + arrives(0)
    grads_across.append(swap_y(clock.passes(grads_own[0])))
    upw.finish(clock)
    inw.start(clock)
    upw.start(clock)
    dgain_mixer = dgain_mixer + arrives(1)
    grads_across.append(swap_y(clock.passes(grads_own[1])))
    grads_near = swap_core(jnp.concatenate(grads_own, axis=0))
    gains = jnp.concatenate([dgain_mixer, dgain_ffn]).reshape(-1, 128)
    small = jnp.concatenate([gains, dkernel.reshape(-1, 128)], axis=0)
    grad_gate = gate.final(clock)
    upw.finish(clock)
    upw.start(clock)
    grads_near = clock.passes(grads_near)
    grads_across[0] = clock.passes(grads_across[0])
    block_across = [swap_y(clock.passes(block_own[:sub]))]
    inw.finish(clock)
    down.start(clock)
    inw.start(clock)
    seq_bits = range(log_two(lax.axis_size("seq")))
    small = clock.passes(small)
    small_came = swap(small, "seq", 1)
    grad_upw = upw.final(clock)
    grads_across[1] = clock.passes(grads_across[1])
    block_across.append(swap_y(clock.passes(block_own[sub:])))
    inw.finish(clock)
    inw.start(clock)
    for bit in seq_bits:
        small = small + clock.passes(small_came)
        if bit + 1 < len(seq_bits):
            small_came = swap(small, "seq", 2 << bit)
        if bit == 0:
            down.finish(clock)
            outw.start(clock)
            down.start(clock)
    grads_corner = swap_core(jnp.concatenate(grads_across, axis=0))
    grad_in = inw.final(clock)
    block_across[0] = clock.passes(block_across[0])
    outw.finish(clock)
    outw.start(clock)
    gains = sum_all(small[: gains.shape[0]], "tp").reshape(2, features)
    dkernel = small[gains.size // 128 :].reshape(dkernel.shape)
    grad_down = down.final(clock)
    block_near = swap_core(clock.passes(block_own))
    grad_tokens = place_rows(
        [*grads_own, grads_near, *grads_across, clock.passes(grads_corner)],
        [piece(k, j, w) for k in (upper, 1 - upper) for w in (core, 1 - core) for j in range(2)],
        sub,
        count,
        jnp.float32,
    )
    outw.finish(clock)
    outw.start(clock)
    block_near = clock.passes(block_near)
    block_across[1] = clock.passes(block_across[1])
    block_corner = swap_core(jnp.concatenate(block_across, axis=0))
    grad_outw_both = outw.final(clock)
    grad_outw = grad_outw_both[:, :quarter] + swap_y(grad_outw_both[:, quarter:])
    grad_outw = lax.optimization_barrier(grad_outw.T)
    grad_down = lax.optimization_barrier(grad_down.T)
    block_out = place_rows(
        [block_own, block_near, *block_across, block_corner],
        [piece(k, j, w) for k in (upper, 1 - upper) for w in (core, 1 - core) for j in range(2)],
        sub,
        count,
        jnp.bfloat16,
    )

    width = features // lax.axis_size("seq")

    def rows_of(weight):
        return lax.dynamic_slice_in_dim(weight, place * width, width, 0).astype(jnp.float32)

    def columns_of(weight):
        return lax.dynamic_slice_in_dim(weight, place * width, width, 1).astype(jnp.float32)

    params = [
        clock.value,
        rows_of(w_bgate),
        rows_of(w_cgate),
        rows_of(w_input),
        kernel,
        columns_of(w_output),
        gain_ffn,
        rows_of(w_gate),
        rows_of(w_up),
        columns_of(w_down),
    ]
    grads = [
        gains[0],
        grad_in[:, :quarter],
        grad_in[:, quarter : 2 * quarter],
        grad_in[:, 2 * quarter :],
        dkernel,
        grad_outw,
        gains[1],
        grad_gate,
        grad_upw,
        grad_down,
    ]
    moments = [
        (mean_gain_mixer, square_gain_mixer),
        (mean_w_bgate, square_w_bgate),
        (mean_w_cgate, square_w_cgate),
        (mean_w_input, square_w_input),
        (mean_conv_kernel, square_conv_kernel),
        (mean_w_output, square_w_output),
        (mean_gain_ffn, square_gain_ffn),
        (mean_w_gate, square_w_gate),
        (mean_w_up, square_w_up),
        (mean_w_down, square_w_down),
    ]
    decays = [0.0, 0.1, 0.1, 0.1, 0.1, 0.1, 0.0, 0.1, 0.1, 0.1]
    rates = [0.2, 0.01, 0.01, 0.01, 0.2, 0.01, 0.2, 0.01, 0.01, 0.01]
    outs = [block_out, grad_tokens]
    for index in range(10):
        weight_new, mean_new, square_new = adamw(
            params[index],
            grads[index],
            moments[index][0],
            moments[index][1],
            decays[index],
            rates[index],
        )
        outs = outs + [grads[index], weight_new, mean_new, square_new]
    return tuple(outs)


def solution(mesh):
    in_specs = (
        P("seq", None),
        P("seq", None),
        P("seq"),
        P(),
        P(None, "tp"),
        P(None, "tp"),
        P(None, "tp"),
        P(None, "tp"),
        P("tp", None),
        P(),
        P(None, "tp"),
        P(None, "tp"),
        P("tp", None),
        P(),
        P(),
        P("seq", "tp"),
        P("seq", "tp"),
        P("seq", "tp"),
        P("seq", "tp"),
        P("seq", "tp"),
        P("seq", "tp"),
        P(None, "tp"),
        P(None, "tp"),
        P("tp", "seq"),
        P("tp", "seq"),
        P(),
        P(),
        P("seq", "tp"),
        P("seq", "tp"),
        P("seq", "tp"),
        P("seq", "tp"),
        P("tp", "seq"),
        P("tp", "seq"),
    )
    out_specs = (
        P("seq", None),
        P("seq", None),
        P(),
        P(),
        P(),
        P(),
        P("seq", "tp"),
        P("seq", "tp"),
        P("seq", "tp"),
        P("seq", "tp"),
        P("seq", "tp"),
        P("seq", "tp"),
        P("seq", "tp"),
        P("seq", "tp"),
        P("seq", "tp"),
        P("seq", "tp"),
        P("seq", "tp"),
        P("seq", "tp"),
        P(None, "tp"),
        P(None, "tp"),
        P(None, "tp"),
        P(None, "tp"),
        P("tp", "seq"),
        P("tp", "seq"),
        P("tp", "seq"),
        P("tp", "seq"),
        P(),
        P(),
        P(),
        P(),
        P("seq", "tp"),
        P("seq", "tp"),
        P("seq", "tp"),
        P("seq", "tp"),
        P("seq", "tp"),
        P("seq", "tp"),
        P("seq", "tp"),
        P("seq", "tp"),
        P("tp", "seq"),
        P("tp", "seq"),
        P("tp", "seq"),
        P("tp", "seq"),
    )
    return jax.shard_map(body, mesh=mesh, in_specs=in_specs, out_specs=out_specs, check_vma=False)
```

```python
import functools

import jax
import jax.numpy as jnp
from jax import lax
from jax.experimental import pallas as pl
from jax.experimental.pallas import tpu as pltpu
from jax.sharding import PartitionSpec as P

EPS = 1e-05


def shifted(block, axis, distance):
    devices = range(lax.axis_size(axis))
    route = [(i - distance, i) for i in devices if i - distance in devices]
    return lax.ppermute(block, axis, route)


def swap(block, axis, bit):
    return lax.ppermute(block, axis, [(i, i ^ bit) for i in range(lax.axis_size(axis))])


def swap_core(block):
    return swap(block, "tp", 1)


def swap_core_halves(block):
    size = block.shape[0] // 2
    return jnp.concatenate([swap_core(block[:size]), swap_core(block[size:])], axis=0)


class Clock:
    def __init__(self, value):
        self.value = value

    def passes(self, *values):
        values, self.value = lax.optimization_barrier((values, self.value))
        return values if len(values) > 1 else values[0]


def swap_y(block):
    return swap(block, "tp", 2)


def narrow(block):
    one = 1.0 + (lax.axis_index("tp") // lax.axis_size("tp")).astype(jnp.float32)
    return (block * one).astype(jnp.bfloat16)


def wide(block):
    return block.astype(jnp.float32)


def dot(left, right):
    return jnp.dot(left, right, preferred_element_type=jnp.float32)


def inner_rows(left, right):
    return lax.dot_general(
        left, right, (((0,), (0,)), ((), ())), preferred_element_type=jnp.float32
    )


def times_back(left, right):
    return lax.dot_general(
        left, right, (((1,), (1,)), ((), ())), preferred_element_type=jnp.float32
    )


def adamw(weight, grad, mean, square, decay, rate):
    mean_new = 0.9 * mean + 0.1 * grad
    square_new = 0.95 * square + 0.05 * grad * grad
    mean_hat = mean_new / (1.0 - 0.9**3)
    square_hat = square_new / (1.0 - 0.95**3)
    weight_new = weight - rate * (mean_hat / (jnp.sqrt(square_hat) + 1e-08) + decay * weight)
    return (weight_new, mean_new, square_new)


def turned_kernel(decay, rate, turned, weight, mean, square, *outs):
    grad = turned[...].T
    updated = adamw(weight[...].astype(jnp.float32), grad, mean[...], square[...], decay, rate)
    for out, value in zip(outs, (grad,) + updated):
        out[...] = value


def adamw_turned(turned, weight, mean, square, decay, rate):
    if mean.shape[1] % 128 != 0:
        grad = turned.T
        return (grad,) + adamw(weight.astype(jnp.float32), grad, mean, square, decay, rate)
    return pl.pallas_call(
        functools.partial(turned_kernel, decay, rate),
        out_shape=[jax.ShapeDtypeStruct(mean.shape, jnp.float32)] * 4,
        compiler_params=pltpu.CompilerParams(vmem_limit_bytes=24 * 2**20),
        cost_estimate=pl.CostEstimate(flops=10**9, bytes_accessed=10**7, transcendentals=0),
    )(turned, weight, mean, square)


def norm_back(dnormed, normed, inverse):
    return inverse * (dnormed - normed * jnp.mean(dnormed * normed, axis=-1, keepdims=True))


def log_two(number):
    bits = number.bit_length() - 1
    assert number == 1 << bits
    return bits


def ffn_kernel(count, place, *refs):
    pieces, (cotangent, *weights) = refs[:count], refs[count : count + 4]
    outs, scratch = refs[-15:-7], refs[-7:]
    htwo_out, act_out, dgate_out, dup_out, fkeep, fsend, dkeep, dsend = outs
    w_gate, w_up, w_down, cots, htwo, weight_sems, cot_sems = scratch
    step = pl.program_id(0)
    size = htwo.shape[0]
    copies = [
        pltpu.make_async_copy(source, target, weight_sems.at[k])
        for k, (source, target) in enumerate(zip(weights, (w_gate, w_up, w_down)))
    ]

    def cot_copy(index):
        rows = pl.ds(pl.multiple_of(place[index] * size, size), size)
        slot = index % 2
        return pltpu.make_async_copy(cotangent.at[rows], cots.at[slot], cot_sems.at[slot])

    @pl.when(step == 0)
    def _():
        copies[0].start()
        copies[1].start()
        cot_copy(0).start()
        copies[2].start()

    @pl.when(step + 1 < count)
    def _():
        cot_copy(step + 1).start()

    for k, ref in enumerate(pieces):

        @pl.when(step == k)
        def _(ref=ref):
            htwo[...] = ref[...].astype(jnp.bfloat16)

    htwo_out[...] = htwo[...]

    @pl.when(step == 0)
    def _():
        copies[0].wait()

    gate = dot(htwo[...], w_gate[...])

    @pl.when(step == 0)
    def _():
        copies[1].wait()

    upval = dot(htwo[...], w_up[...])
    cot_copy(step).wait()

    @pl.when(step == 0)
    def _():
        copies[2].wait()

    dact = times_back(cots[step % 2], w_down[...])
    sigma = jax.nn.sigmoid(gate)
    silu_gate = gate * sigma
    act = (silu_gate * upval).astype(jnp.bfloat16)
    dgate = (dact * upval * (sigma * (1.0 + gate * (1.0 - sigma)))).astype(jnp.bfloat16)
    dup = (dact * silu_gate).astype(jnp.bfloat16)
    act_out[...] = act
    dgate_out[...] = dgate
    dup_out[...] = dup
    dhtwo = times_back(dgate, w_gate[...]) + times_back(dup, w_up[...])
    ffn = dot(act, w_down[...])

    @pl.when(step % 2 == 0)
    def _():
        fkeep[...] = ffn
        dkeep[...] = dhtwo

    @pl.when(step % 2 == 1)
    def _():
        fsend[...] = ffn
        dsend[...] = dhtwo


def feed_forward(place, pieces, cotangent, weights, kept):
    features = cotangent.shape[1]
    size = pieces[0].shape[0]
    units = weights[0].shape[1]
    whole = lambda ref: pl.BlockSpec(ref.shape, lambda i, p: (0, 0), pipeline_mode=pl.Buffered(1))
    spot = lambda width: pl.BlockSpec((size, width), lambda i, p: (p[i], 0))
    part = pl.BlockSpec((size, features), lambda i, p: (i // 2, 0))
    kept = [] if kept is None else list(kept)
    shapes = [
        pltpu.HBM((cotangent.shape[0], width), jnp.bfloat16)
        for width in (features, units, units, units)
    ]
    shapes += [pltpu.HBM((size * len(pieces) // 2, features), jnp.float32)] * 4
    return pl.pallas_call(
        functools.partial(ffn_kernel, len(pieces)),
        grid_spec=pltpu.PrefetchScalarGridSpec(
            num_scalar_prefetch=1,
            grid=(len(pieces),),
            in_specs=[whole(ref) for ref in pieces]
            + [pl.BlockSpec(memory_space=pltpu.HBM)] * 4
            + [pl.BlockSpec(memory_space=pl.ANY)] * len(kept),
            out_specs=[spot(features), spot(units), spot(units), spot(units)] + [part] * 4,
            scratch_shapes=[pltpu.VMEM(w.shape, w.dtype) for w in weights]
            + [
                pltpu.VMEM((2, size, features), cotangent.dtype),
                pltpu.VMEM((size, features), jnp.bfloat16),
                pltpu.SemaphoreType.DMA((3,)),
                pltpu.SemaphoreType.DMA((2,)),
            ],
        ),
        out_shape=shapes,
        input_output_aliases={5 + len(pieces) + i: i for i in range(len(kept))},
        compiler_params=pltpu.CompilerParams(vmem_limit_bytes=57 * 2**20),
        cost_estimate=pl.CostEstimate(flops=3 * 10**10, bytes_accessed=10**7, transcendentals=0),
    )(jnp.stack(place).astype(jnp.int32), *pieces, cotangent, *weights, *kept)


def place_kernel(pieces, spots, *refs):
    out = refs[-1]
    size = out.shape[0]
    for step, (index, part) in enumerate(pieces):

        @pl.when(pl.program_id(0) == step)
        def _(step=step, index=index, part=part):
            out[...] = refs[index][part * size : (part + 1) * size, :].astype(out.dtype)


def place_rows(blocks, spots, size, count, dtype, whole=None):
    width = blocks[0].shape[1]
    held = [] if whole is None else [whole]
    pieces = [(k, i) for k, block in enumerate(blocks) for i in range(block.shape[0] // size)]
    return pl.pallas_call(
        functools.partial(place_kernel, pieces),
        grid_spec=pltpu.PrefetchScalarGridSpec(
            num_scalar_prefetch=1,
            grid=(len(pieces),),
            in_specs=[
                pl.BlockSpec(block.shape, lambda i, p: (0, 0), pipeline_mode=pl.Buffered(1))
                for block in blocks
            ]
            + [pl.BlockSpec(memory_space=pl.ANY)] * len(held),
            out_specs=pl.BlockSpec((size, width), lambda i, p: (p[i], 0)),
        ),
        out_shape=jax.ShapeDtypeStruct((count, width), dtype),
        input_output_aliases={1 + len(blocks): 0} if held else {},
        compiler_params=pltpu.CompilerParams(vmem_limit_bytes=32 * 2**20),
        cost_estimate=pl.CostEstimate(
            flops=0, bytes_accessed=8 * len(pieces) * size * width, transcendentals=0
        ),
    )(jnp.stack(spots).astype(jnp.int32), *blocks, *held)


def sum_kernel(wide_rows, parts, picks, *refs):
    right, send, keep = refs[parts], refs[-2], refs[-1]
    left = jnp.concatenate([ref[...] for ref in refs[:parts]], axis=1)
    total = inner_rows(left, right[...])

    @pl.when(pl.program_id(0) == 0)
    def _():
        send[...] = total

    @pl.when(pl.program_id(0) == 1)
    def _():
        keep[...] = total


def sum_halves(left, right, place, bit):
    shards = lax.axis_size("seq")
    width = left.shape[1] // shards
    parts = shards // 2
    mine = (place >> bit) & 1
    low = jnp.arange(parts, dtype=jnp.int32)
    low, high = low & ((1 << bit) - 1), low >> bit
    base = (high << (bit + 1)) | low
    picks = jnp.concatenate([base | ((1 - mine) << bit), base | (mine << bit)]).astype(jnp.int32)
    if width % 128 != 0:
        total = inner_rows(left, right).reshape(-1, 2, 1 << bit, width * right.shape[1])
        return tuple(
            lax.dynamic_index_in_dim(total, which, 1, keepdims=False).reshape(-1, right.shape[1])
            for which in (1 - mine, mine)
        )
    count, units = right.shape
    half = jax.ShapeDtypeStruct((parts * width, units), jnp.float32)
    pick = lambda k: pl.BlockSpec((count, width), lambda i, p, k=k: (0, p[i * parts + k]))
    fixed = lambda shape: pl.BlockSpec(shape, lambda i, p: (0, 0), pipeline_mode=pl.Buffered(1))
    return pl.pallas_call(
        functools.partial(sum_kernel, width, parts),
        grid_spec=pltpu.PrefetchScalarGridSpec(
            num_scalar_prefetch=1,
            grid=(2,),
            in_specs=[pick(k) for k in range(parts)] + [fixed(right.shape)],
            out_specs=[fixed(half.shape)] * 2,
        ),
        out_shape=[pltpu.HBM(half.shape, half.dtype)] * 2,
        compiler_params=pltpu.CompilerParams(vmem_limit_bytes=57 * 2**20),
        cost_estimate=pl.CostEstimate(flops=10**12, bytes_accessed=10**7, transcendentals=0),
    )(picks, *[left] * parts, right)


def step_kernel(picks, *refs):
    keep_one, came_one, keep_two, came_two, send, keep = refs
    send[...] = keep_one[...] + came_one[...]
    keep[...] = keep_two[...] + came_two[...]


def halve_sum(kept, came, mine, low):
    blocks, width, units = kept.shape
    if width % 8 != 0 or units % 128 != 0:
        pairs = (kept + came).reshape(-1, 2, low, width, units)
        return tuple(
            lax.dynamic_index_in_dim(pairs, which, 1, keepdims=False).reshape(-1, width, units)
            for which in (1 - mine, mine)
        )
    index = jnp.arange(blocks // 2, dtype=jnp.int32)
    base = (index // low) * (2 * low) + index % low
    picks = jnp.concatenate([base + (1 - mine) * low, base + mine * low]).astype(jnp.int32)
    one = pl.BlockSpec((1, width, units), lambda i, p: (p[i], 0, 0))
    two = pl.BlockSpec((1, width, units), lambda i, p: (p[i + blocks // 2], 0, 0))
    half = pl.BlockSpec((1, width, units), lambda i, p: (i, 0, 0))
    return pl.pallas_call(
        step_kernel,
        grid_spec=pltpu.PrefetchScalarGridSpec(
            num_scalar_prefetch=1,
            grid=(blocks // 2,),
            in_specs=[one, one, two, two],
            out_specs=[half, half],
        ),
        out_shape=[jax.ShapeDtypeStruct((blocks // 2, width, units), kept.dtype)] * 2,
        cost_estimate=pl.CostEstimate(flops=10**12, bytes_accessed=10**7, transcendentals=0),
    )(picks, kept, came, kept, came)


class Halving:
    def __init__(self, clock, left, right, place, order):
        shards = lax.axis_size("seq")
        self.shape = (left.shape[1] // shards, right.shape[1])
        self.place = place
        self.order = list(order)
        self.left = list(range(log_two(shards)))
        left, right = clock.passes(left, right)
        send, keep = clock.passes(*sum_halves(left, right, place, order[0]))
        self.send, self.keep = send.reshape((-1,) + self.shape), keep.reshape((-1,) + self.shape)

    def start(self, clock=None):
        bit = self.order.pop(0)
        self.left.remove(bit)
        send = self.send if clock is None else clock.passes(self.send)
        self.came = swap(send, "seq", 1 << bit)

    def finish(self, clock):
        came = clock.passes(self.came)
        if not self.order:
            self.total = self.keep + came
            return
        bit = self.order[0]
        low = 1 << self.left.index(bit)
        self.send, self.keep = halve_sum(self.keep, came, (self.place >> bit) & 1, low)

    def final(self, clock):
        self.finish(clock)
        while self.order:
            self.start()
            self.finish(clock)
        return self.total[0]


def sum_all(block, axis):
    for bit in range(log_two(lax.axis_size(axis))):
        block = block + swap(block, axis, 1 << bit)
    return block


def body(
    tokens,
    cotangent,
    start_flags,
    gain_mixer,
    w_bgate,
    w_cgate,
    w_input,
    conv_kernel,
    w_output,
    gain_ffn,
    w_gate,
    w_up,
    w_down,
    mean_gain_mixer,
    square_gain_mixer,
    mean_w_bgate,
    square_w_bgate,
    mean_w_cgate,
    square_w_cgate,
    mean_w_input,
    square_w_input,
    mean_conv_kernel,
    square_conv_kernel,
    mean_w_output,
    square_w_output,
    mean_gain_ffn,
    square_gain_ffn,
    mean_w_gate,
    square_w_gate,
    mean_w_up,
    square_w_up,
    mean_w_down,
    square_w_down,
):
    count, features = tokens.shape
    half = count // 2
    part = count // 4
    sub = count // 8
    place = lax.axis_index("seq")
    rank = lax.axis_index("tp")
    upper = rank // 2
    core = rank % 2
    near_first = list(range(log_two(lax.axis_size("seq"))))
    far_first = [near_first[1], near_first[0]] + near_first[2:]
    quarter = w_output.shape[0]

    def rows(block, index, size):
        return lax.dynamic_slice_in_dim(block, index * size, size, 0)

    def piece(chip, j, which):
        return chip * 4 + j * 2 + which

    def joined(mine, other):
        return jnp.where(
            core == 0,
            jnp.concatenate([mine, other], axis=0),
            jnp.concatenate([other, mine], axis=0),
        )

    clock = Clock(gain_mixer)
    w_output_far = narrow(swap_y(wide(w_output)))
    w_output_both = jnp.concatenate([w_output, w_output_far], axis=0)
    xin = tokens.astype(jnp.float32)
    inverse_one = lax.rsqrt(jnp.mean(xin * xin, axis=-1, keepdims=True) + EPS)
    norm_one = xin * inverse_one
    hone = (norm_one * gain_mixer).astype(jnp.bfloat16)
    last = hone[-8:]
    mixed_last = dot(last, w_bgate) * dot(last, w_input)
    cgate_next = shifted(dot(hone[:8], w_cgate), "seq", -1)
    keeper = (1 - start_flags[0]).astype(jnp.float32)
    kernel = conv_kernel.astype(jnp.float32)
    previous = shifted(mixed_last, "seq", 1)[-2:] * keeper
    bgate = dot(hone, w_bgate)
    cgate = dot(hone, w_cgate)
    xval = dot(hone, w_input)
    mixed_in = bgate * xval
    extended = jnp.concatenate([previous, mixed_in], axis=0)
    conv = kernel[2] * mixed_in + kernel[1] * extended[1:-1] + kernel[0] * extended[:-2]
    gated = (cgate * conv).astype(jnp.bfloat16)

    gated_both, resid, norm_two, inverse_two, htwo_own, htwo_near = [], [], [], [], [], []
    htwo_across = []
    w_all = jnp.concatenate([w_bgate, w_cgate, w_input], axis=1)
    x_own = [
        rows(tokens, piece(upper, j, core), sub).astype(jnp.float32) for j in range(2)
    ]
    inverse_own = [
        lax.rsqrt(jnp.mean(x * x, axis=-1, keepdims=True) + EPS) for x in x_own
    ]
    far = swap_y(wide(rows(gated, 1 - upper, half)))
    w_all = jnp.concatenate([w_all, narrow(swap_core(wide(w_all)))], axis=1)
    w_all, inverse_own, w_output_far, w_output_both, cgate_next = clock.passes(
        w_all, inverse_own, w_output_far, w_output_both, cgate_next
    )
    far = clock.passes(far)
    fars = [far[:part], far[part:]]
    for j in range(2):
        both = jnp.concatenate([rows(gated, upper * 2 + j, part), narrow(fars[j])], axis=1)
        gated_both.append(both)
        mix_send = dot(rows(both, 1 - core, sub), w_output_both)
        mix_keep = dot(rows(both, core, sub), w_output_both)
        resid.append(x_own[j] + (mix_keep + swap_core(mix_send)))
        inverse_two.append(
            lax.rsqrt(jnp.mean(resid[j] * resid[j], axis=-1, keepdims=True) + EPS)
        )
        norm_two.append(resid[j] * inverse_two[j])
        htwo_own.append(wide((norm_two[j] * gain_ffn).astype(jnp.bfloat16)))
        htwo_across.append(swap_y(htwo_own[j]))
        htwo_near.append(swap_core(htwo_own[j]))

    weights = (w_gate, w_up, w_down)
    spots = [piece(upper, j, which) for j in range(2) for which in (core, 1 - core)]
    pieces = [v for j in range(2) for v in (htwo_own[j], htwo_near[j])]
    outs = clock.passes(*feed_forward(spots, pieces, cotangent, weights, None))
    kept, ffn_here, dhtwo_here = outs[:4], outs[4:6], outs[6:]
    ffn_there, dhtwo_across = [], []
    dhtwo_here = dhtwo_here[0] + swap_core(dhtwo_here[1])
    for j in range(2):
        if j == 1:
            dhtwo_here = clock.passes(dhtwo_here)
        across = clock.passes(htwo_across[j])
        spots = [piece(1 - upper, j, which) for which in (core, 1 - core)]
        pieces = [across, swap_core(across)]
        outs = clock.passes(*feed_forward(spots, pieces, cotangent, weights, kept))
        kept = outs[:4]
        ffn_there.append(outs[4:6])
        dhtwo_across.append(swap_y(clock.passes(outs[6] + swap_core_halves(outs[7]))))
    htwo_all, act_all, dgate_all, dup_all = kept
    def to_previous(block, chip):
        ranks = lax.axis_size("tp")
        route = [
            (s * ranks + c, (s - 1) * ranks + 2 * chip + c)
            for s in range(1, lax.axis_size("seq"))
            for c in range(2)
        ]
        return lax.ppermute(block, ("seq", "tp"), route)

    dresid, dgain_ffn, dmix, dgated_near, dgated_far = [], 0.0, [], [], []

    def before_swap(j):
        gout = rows(cotangent, piece(upper, j, core), sub).astype(jnp.float32)
        dhtwo = dhtwo_here[j * sub : (j + 1) * sub] + clock.passes(dhtwo_across[j])
        dresid.append(gout + norm_back(dhtwo * gain_ffn, norm_two[j], inverse_two[j]))
        dmix_own = clock.passes(wide(dresid[j].astype(jnp.bfloat16)))
        return dmix_own, swap_core(dmix_own), jnp.sum(dhtwo * norm_two[j], axis=0)

    def after_swap(dmix_own, came):
        dmix.append(narrow(joined(dmix_own, clock.passes(came))))
        near, far = clock.passes(
            times_back(dmix[-1], w_output), times_back(dmix[-1], w_output_far)
        )
        dgated_near.append(near)
        dgated_far.append(swap_y(far))
        return near, far

    def ffn_sum(j):
        keep, send = clock.passes(*ffn_there[j])
        return keep + swap_core(send)

    dmix_own, came, gain_part = before_swap(0)
    dgain_ffn = dgain_ffn + gain_part
    down = Halving(clock, cotangent, act_all, place, far_first)
    near, far = after_swap(dmix_own, came)
    dgated_next = to_previous(near[:8] * keeper, 0) + to_previous(far[:8] * keeper, 1)
    gate = Halving(clock, htwo_all, dgate_all, place, near_first)
    down.start(clock)
    gate.start(clock)
    dgated_next = clock.passes(dgated_next)
    dmix_own, came, gain_part = before_swap(1)
    dgain_ffn = dgain_ffn + gain_part
    dgated_far[0] = clock.passes(dgated_far[0])
    ffn_far = [ffn_sum(j) for j in range(2)]
    upw = Halving(clock, htwo_all, dup_all, place, near_first)
    after_swap(dmix_own, came)
    ffn_across = [swap_y(clock.passes(block)) for block in ffn_far]
    outw = Halving(
        clock,
        jnp.concatenate(dmix, axis=0),
        jnp.concatenate(gated_both, axis=0),
        place,
        near_first,
    )
    dgated_far[1] = clock.passes(dgated_far[1])
    dgated = jnp.where(
        upper == 0,
        jnp.concatenate(dgated_near + dgated_far, axis=0),
        jnp.concatenate(dgated_far + dgated_near, axis=0),
    )

    dcgate = (dgated * conv).astype(jnp.bfloat16)
    dconv = dgated * cgate
    dkernel = jnp.stack(
        [
            jnp.sum(dconv * extended[:-2], axis=0),
            jnp.sum(dconv * extended[1:-1], axis=0),
            jnp.sum(dconv * mixed_in, axis=0),
        ],
        axis=0,
    )
    dextended = (
        jnp.pad(kernel[2] * dconv, ((2, 0), (0, 0)))
        + jnp.pad(kernel[1] * dconv, ((1, 1), (0, 0)))
        + jnp.pad(kernel[0] * dconv, ((0, 2), (0, 0)))
    )
    dconv_next = dgated_next[:2] * cgate_next[:2]
    returned = jnp.concatenate(
        [kernel[0] * dconv_next[:1], kernel[1] * dconv_next[:1] + kernel[0] * dconv_next[1:]],
        axis=0,
    )
    dmixed = dextended[2:] + jnp.pad(returned, ((count - 2, 0), (0, 0)))
    dbgate = (dmixed * xval).astype(jnp.bfloat16)
    dxval = (dmixed * bgate).astype(jnp.bfloat16)
    dall = jnp.concatenate([dbgate, dcgate, dxval], axis=1)
    by_core = dall.reshape(4, 2, sub, dall.shape[1])
    send = lax.dynamic_index_in_dim(by_core, 1 - core, 1, keepdims=False)
    came = swap_core(clock.passes(wide(send)))
    down.finish(clock)
    gate.finish(clock)
    upw.start(clock)
    gate.start(clock)
    inw = Halving(clock, hone, dall, place, near_first)
    came = clock.passes(came)
    ffn_here = clock.passes(*ffn_here)
    ffn_near = swap_core(ffn_here[1])
    dall_own = lax.dynamic_index_in_dim(by_core, core, 1, keepdims=False)
    dall_own = jnp.concatenate([dall_own, narrow(came)], axis=2)

    def back_rows(chip, j):
        block = lax.dynamic_index_in_dim(dall_own, chip * 2 + j, 0, keepdims=False)
        return times_back(block, w_all)

    dhone_across = [swap_y(clock.passes(back_rows(1 - upper, j))) for j in range(2)]
    dhone_near = [back_rows(upper, j) for j in range(2)]

    ffn_across[0] = clock.passes(ffn_across[0])
    gate.finish(clock)
    gate.start(clock)
    ffn_near = ffn_here[0] + clock.passes(ffn_near)
    dgain_mixer, grads_own, grads_across = 0.0, [], []

    def arrives(j):
        norm_own = x_own[j] * inverse_own[j]
        dhone = dhone_near[j] + clock.passes(dhone_across[j])
        grad_own = dresid[j] + norm_back(dhone * gain_mixer, norm_own, inverse_own[j])
        grads_own.append(grad_own)
        return jnp.sum(dhone * norm_own, axis=0)

    ffn_across[1] = clock.passes(ffn_across[1])
    ffn = ffn_near + jnp.concatenate(ffn_across, axis=0)
    block_own = wide((jnp.concatenate(resid, axis=0) + ffn).astype(jnp.bfloat16))
    dgain_mixer = dgain_mixer + arrives(0)
    grads_across.append(swap_y(clock.passes(grads_own[0])))
    upw.finish(clock)
    inw.start(clock)
    upw.start(clock)
    dgain_mixer = dgain_mixer + arrives(1)
    grads_across.append(swap_y(clock.passes(grads_own[1])))
    grads_near = swap_core(jnp.concatenate(grads_own, axis=0))
    gains = jnp.concatenate([dgain_mixer, dgain_ffn]).reshape(-1, 128)
    small = jnp.concatenate([gains, dkernel.reshape(-1, 128)], axis=0)
    grad_gate = gate.final(clock)
    upw.finish(clock)
    upw.start(clock)
    grads_near = clock.passes(grads_near)
    grads_across[0] = clock.passes(grads_across[0])
    block_across = [swap_y(clock.passes(block_own[:sub]))]
    inw.finish(clock)
    down.start(clock)
    inw.start(clock)
    seq_bits = range(log_two(lax.axis_size("seq")))
    small = clock.passes(small)
    small_came = swap(small, "seq", 1)
    grad_upw = upw.final(clock)
    grads_across[1] = clock.passes(grads_across[1])
    block_across.append(swap_y(clock.passes(block_own[sub:])))
    inw.finish(clock)
    inw.start(clock)
    for bit in seq_bits:
        small = small + clock.passes(small_came)
        if bit + 1 < len(seq_bits):
            small_came = swap(small, "seq", 2 << bit)
        if bit == 0:
            down.finish(clock)
            outw.start(clock)
            down.start(clock)
    grads_corner = swap_core(jnp.concatenate(grads_across, axis=0))
    grad_in = inw.final(clock)
    block_across[0] = clock.passes(block_across[0])
    outw.finish(clock)
    outw.start(clock)
    gains = sum_all(small[: gains.shape[0]], "tp").reshape(2, features)
    dkernel = small[gains.size // 128 :].reshape(dkernel.shape)
    grad_down = down.final(clock)
    block_near = swap_core(clock.passes(block_own))
    grad_tokens = place_rows(
        [*grads_own, grads_near, *grads_across, clock.passes(grads_corner)],
        [piece(k, j, w) for k in (upper, 1 - upper) for w in (core, 1 - core) for j in range(2)],
        sub,
        count,
        jnp.float32,
    )
    grad_tokens = clock.passes(grad_tokens)
    outw.finish(clock)
    outw.start(clock)
    block_near = clock.passes(block_near)
    block_across[1] = clock.passes(block_across[1])
    block_corner = clock.passes(swap_core(jnp.concatenate(block_across, axis=0)))
    block_out = place_rows(
        [block_own, block_near, *block_across, block_corner],
        [piece(k, j, w) for k in (upper, 1 - upper) for w in (core, 1 - core) for j in range(2)],
        sub,
        count,
        jnp.bfloat16,
    )
    block_out = clock.passes(block_out)
    grad_outw_both = outw.final(clock)
    grad_outw = grad_outw_both[:, :quarter] + swap_y(grad_outw_both[:, quarter:])

    width = features // lax.axis_size("seq")

    def rows_of(weight):
        return lax.dynamic_slice_in_dim(weight, place * width, width, 0).astype(jnp.float32)

    params = [
        clock.value,
        rows_of(w_bgate),
        rows_of(w_cgate),
        rows_of(w_input),
        kernel,
        None,
        gain_ffn,
        rows_of(w_gate),
        rows_of(w_up),
        None,
    ]
    grads = [
        gains[0],
        grad_in[:, :quarter],
        grad_in[:, quarter : 2 * quarter],
        grad_in[:, 2 * quarter :],
        dkernel,
        grad_outw,
        gains[1],
        grad_gate,
        grad_upw,
        grad_down,
    ]
    moments = [
        (mean_gain_mixer, square_gain_mixer),
        (mean_w_bgate, square_w_bgate),
        (mean_w_cgate, square_w_cgate),
        (mean_w_input, square_w_input),
        (mean_conv_kernel, square_conv_kernel),
        (mean_w_output, square_w_output),
        (mean_gain_ffn, square_gain_ffn),
        (mean_w_gate, square_w_gate),
        (mean_w_up, square_w_up),
        (mean_w_down, square_w_down),
    ]
    decays = [0.0, 0.1, 0.1, 0.1, 0.1, 0.1, 0.0, 0.1, 0.1, 0.1]
    rates = [0.2, 0.01, 0.01, 0.01, 0.2, 0.01, 0.2, 0.01, 0.01, 0.01]
    outs = [block_out, grad_tokens]
    for index in range(10):
        mean, square = moments[index]
        if index in (5, 9):
            weight = lax.dynamic_slice_in_dim(
                w_output if index == 5 else w_down, place * width, width, 1
            )
            outs += list(
                adamw_turned(grads[index], weight, mean, square, decays[index], rates[index])
            )
            continue
        updated = adamw(params[index], grads[index], mean, square, decays[index], rates[index])
        outs += [grads[index], *updated]
    return tuple(outs)


def solution(mesh):
    in_specs = (
        P("seq", None),
        P("seq", None),
        P("seq"),
        P(),
        P(None, "tp"),
        P(None, "tp"),
        P(None, "tp"),
        P(None, "tp"),
        P("tp", None),
        P(),
        P(None, "tp"),
        P(None, "tp"),
        P("tp", None),
        P(),
        P(),
        P("seq", "tp"),
        P("seq", "tp"),
        P("seq", "tp"),
        P("seq", "tp"),
        P("seq", "tp"),
        P("seq", "tp"),
        P(None, "tp"),
        P(None, "tp"),
        P("tp", "seq"),
        P("tp", "seq"),
        P(),
        P(),
        P("seq", "tp"),
        P("seq", "tp"),
        P("seq", "tp"),
        P("seq", "tp"),
        P("tp", "seq"),
        P("tp", "seq"),
    )
    out_specs = (
        P("seq", None),
        P("seq", None),
        P(),
        P(),
        P(),
        P(),
        P("seq", "tp"),
        P("seq", "tp"),
        P("seq", "tp"),
        P("seq", "tp"),
        P("seq", "tp"),
        P("seq", "tp"),
        P("seq", "tp"),
        P("seq", "tp"),
        P("seq", "tp"),
        P("seq", "tp"),
        P("seq", "tp"),
        P("seq", "tp"),
        P(None, "tp"),
        P(None, "tp"),
        P(None, "tp"),
        P(None, "tp"),
        P("tp", "seq"),
        P("tp", "seq"),
        P("tp", "seq"),
        P("tp", "seq"),
        P(),
        P(),
        P(),
        P(),
        P("seq", "tp"),
        P("seq", "tp"),
        P("seq", "tp"),
        P("seq", "tp"),
        P("seq", "tp"),
        P("seq", "tp"),
        P("seq", "tp"),
        P("seq", "tp"),
        P("tp", "seq"),
        P("tp", "seq"),
        P("tp", "seq"),
        P("tp", "seq"),
    )
    return jax.shard_map(body, mesh=mesh, in_specs=in_specs, out_specs=out_specs, check_vma=False)
```
